512 devices in a mesh: row: 32 (over x, y), col: 16 (over z, core).
Axes of the slice: x: 4, y: 8, z: 8, core: 2. Of those that a mesh axis runs over, the one named last changes fastest.
Arguments:
- activations: bfloat16 [512, 8192], P('row', 'col'), may hold values from -6 to 6
- out_grad: bfloat16 [512, 8192], P('row', 'col'), may hold values from -1.5 to 1.5
- w_gate: bfloat16 [8192, 14336], P('col', 'row'), may hold values from -0.0625 to 0.0625
- w_up: bfloat16 [8192, 14336], P('col', 'row'), may hold values from -0.0625 to 0.0625
- w_down: bfloat16 [14336, 8192], P('row', 'col'), may hold values from -0.046875 to 0.046875
Outputs:
- in_grad: bfloat16 [512, 8192], P('row', 'col')
- grad_gate: bfloat16 [8192, 14336], P('col', 'row')
- grad_up: bfloat16 [8192, 14336], P('col', 'row')
- grad_down: bfloat16 [14336, 8192], P('row', 'col')
The draws below stay inside these ranges and needn't reach their ends.
All inputs are finite; a program needn't handle non-finite values.
Results may differ from the reference program's by a relative error of at most 0.0049.
Values may be sent and summed in bfloat16 or wider, within the bound.
No kernel may reach another device: no remote copies, remote signals or barrier semaphores. Data moves between devices by JAX's collectives and lax.ppermute only.
A program may use at most 64 MiB of HBM per device.

```python
import jax
import jax.numpy as jnp
from jax import lax

D = 8192
FF = 14336
TOKENS = 512


def raised(array, own_key, source, target, shards_of, factor):
    def block_of(axis_at):
        return (jnp.arange(array.shape[axis_at]) // (array.shape[axis_at] // shards_of)).reshape((-1,) + (1,) * (array.ndim - 1 - axis_at))

    one_side = jax.random.permutation(own_key, shards_of)[block_of(target)]
    other_side = (block_of(target) + shards_of // 2) % shards_of
    return jnp.where((block_of(source) == one_side) | (block_of(source) == other_side), factor * array, array)


def block_scale(own_key, dims, cuts, smallest, largest):
    factor_of = 1.0
    for dim, parts in cuts:
        heights = jax.random.uniform(jax.random.fold_in(jax.random.fold_in(own_key, 6), dim), (parts,), jnp.float32, smallest / len(cuts), largest / len(cuts))
        factor_of = factor_of * jnp.repeat(jnp.exp(heights), dims[dim] // parts).reshape((-1,) + (1,) * (len(dims) - 1 - dim))
    return factor_of


def gaussian(rng, dims, width, reach, pieces=(), kind=jnp.bfloat16):
    drawn = width * jax.random.normal(rng, dims, jnp.float32)
    if pieces:
        drawn = drawn * block_scale(rng, dims, pieces, -0.22, 0.18)
    return jnp.clip(drawn, -reach, reach).astype(kind)


def noise_with(rng, dims, scale, reach, cuts, heavy, kind=jnp.bfloat16):
    array = scale * jax.random.normal(rng, dims, jnp.float32)
    if cuts:
        array = array * block_scale(rng, dims, cuts, -0.22, 0.18)
    return jnp.clip(raised(array, jax.random.fold_in(rng, 3), *heavy), -reach, reach).astype(kind)


def setup_inputs(seed: int = 0) -> dict:
    splits = jax.random.split(jax.random.key(seed), 6)
    return {
        "activations": noise_with(splits[0], (TOKENS, D), 1.0, 6.0, ((0, 32), (1, 16)), (1, 0, 32, 2.75)),
        "out_grad": noise_with(splits[1], (TOKENS, D), 0.25, 1.5, ((0, 32), (1, 16)), (1, 0, 32, 2.75)),
        "w_gate": gaussian(splits[2], (D, FF), D ** -0.5, 0.0625, ((0, 16), (1, 32))),
        "w_up": gaussian(splits[3], (D, FF), D ** -0.5, 0.0625, ((0, 16), (1, 32))),
        "w_down": gaussian(splits[4], (FF, D), FF ** -0.5, 0.046875, ((0, 32), (1, 16))),
    }


def reference(activations, out_grad, w_gate, w_up, w_down):
    contract_last = (((1,), (1,)), ((), ()))
    gate = jnp.dot(activations, w_gate, preferred_element_type=jnp.float32)
    up_val = jnp.dot(activations, w_up, preferred_element_type=jnp.float32)
    hidden_grad = lax.dot_general(out_grad, w_down, contract_last, preferred_element_type=jnp.float32)
    sigma = jax.nn.sigmoid(gate)
    hidden = (gate * sigma * up_val).astype(jnp.bfloat16)
    up_grad = (hidden_grad * gate * sigma).astype(jnp.bfloat16)
    gate_grad = (hidden_grad * up_val * sigma * (1.0 + gate * (1.0 - sigma))).astype(jnp.bfloat16)
    grad_down = jnp.dot(hidden.T, out_grad, preferred_element_type=jnp.float32).astype(jnp.bfloat16)
    grad_gate = jnp.dot(activations.T, gate_grad, preferred_element_type=jnp.float32).astype(jnp.bfloat16)
    grad_up = jnp.dot(activations.T, up_grad, preferred_element_type=jnp.float32).astype(jnp.bfloat16)
    in_sum = lax.dot_general(gate_grad, w_gate, contract_last, preferred_element_type=jnp.float32)
    in_sum = in_sum + lax.dot_general(up_grad, w_up, contract_last, preferred_element_type=jnp.float32)
    return in_sum.astype(jnp.bfloat16), grad_gate, grad_up, grad_down
```

```python
import jax
import jax.numpy as jnp
from jax import lax
from jax.sharding import Mesh
from jax.sharding import PartitionSpec as P

X, Y, Z = 4, 8, 8
ROW = ("x", "y")
COL = ("z", "core")
SWAP = ((0, 1), (1, 0))


def gather(block, axis, count):
    return lax.all_to_all(jnp.broadcast_to(block[None], (count,) + block.shape), axis, 0, 0)


def swiglu_parts(gate, up_val, hidden_grad):
    sigma = jax.nn.sigmoid(gate)
    hidden = (gate * sigma * up_val).astype(jnp.bfloat16)
    up_grad = (hidden_grad * gate * sigma).astype(jnp.bfloat16)
    gate_grad = (hidden_grad * up_val * sigma * (1.0 + gate * (1.0 - sigma))).astype(jnp.bfloat16)
    return jnp.stack([hidden, gate_grad, up_grad])


def product(a, b, contract_a, contract_b):
    return lax.dot_general(
        a, b, (((contract_a,), (contract_b,)), ((), ())), preferred_element_type=jnp.float32
    )


def on_device(activations, out_grad, w_gate, w_up, w_down):
    tokens, width = activations.shape
    units = w_gate.shape[1]
    first = lax.axis_index("core") == 0
    both = gather(jnp.concatenate([activations, out_grad], axis=1), "y", Y)
    both = gather(both.reshape(Y * tokens, 2 * width), "x", X).reshape(X * Y * tokens, 2 * width)
    inputs, grads = both[:, :width], both[:, width:]
    half = inputs.shape[0] // 2

    parts = jnp.stack(
        [product(w_gate, inputs, 0, 1), product(w_up, inputs, 0, 1), product(w_down, grads, 1, 1)]
    )
    low, high = parts[..., :half], parts[..., half:]
    other = lax.ppermute(jnp.where(first, high, low), "core", SWAP)
    chip = (jnp.where(first, low, high) + other).astype(jnp.bfloat16)
    rows = units // Z
    sent = chip.reshape(3, Z, rows, half).transpose(1, 0, 2, 3)
    summed = jnp.sum(lax.all_to_all(sent, "z", 0, 0).astype(jnp.float32), axis=0)

    mine = swiglu_parts(summed[0], summed[1], summed[2])
    own = gather(mine, "z", Z)
    other = lax.ppermute(own, "core", SWAP)
    whole = jnp.where(
        first, jnp.concatenate([own, other], axis=3), jnp.concatenate([other, own], axis=3)
    )
    hidden, gate_grad, up_grad = whole.transpose(1, 0, 2, 3).reshape(3, units, 2 * half)

    term = product(gate_grad, w_gate, 0, 1) + product(up_grad, w_up, 0, 1)
    terms = lax.all_to_all(term.reshape(X * Y, tokens, width), ROW, 0, 0)
    in_grad = jnp.sum(terms, axis=0).astype(jnp.bfloat16)
    grad_down = product(hidden, grads, 1, 0).astype(jnp.bfloat16)
    grad_gate = product(inputs, gate_grad, 0, 1).astype(jnp.bfloat16)
    grad_up = product(inputs, up_grad, 0, 1).astype(jnp.bfloat16)
    return (in_grad, grad_gate, grad_up, grad_down)


def solution(mesh):
    grid = Mesh(mesh.devices.reshape(X, Y, Z, 2), ROW + COL)
    return jax.shard_map(
        on_device,
        mesh=grid,
        in_specs=(P(ROW, COL), P(ROW, COL), P(COL, ROW), P(COL, ROW), P(ROW, COL)),
        out_specs=(P(ROW, COL), P(COL, ROW), P(COL, ROW), P(ROW, COL)),
        check_vma=False,
    )
```

```python
import jax
import jax.numpy as jnp
from jax import lax
from jax.experimental import pallas as pl
from jax.experimental.pallas import tpu as pltpu
from jax.sharding import Mesh
from jax.sharding import PartitionSpec as P

X, Y, Z = 4, 8, 8
ROW = ("x", "y")
COL = ("z", "core")
SWAP = ((0, 1), (1, 0))


def gather(block, axis, count):
    return lax.all_to_all(jnp.broadcast_to(block[None], (count,) + block.shape), axis, 0, 0)


def swiglu_parts(gate, up_val, hidden_grad):
    sigma = jax.nn.sigmoid(gate)
    hidden = (gate * sigma * up_val).astype(jnp.bfloat16)
    up_grad = (hidden_grad * gate * sigma).astype(jnp.bfloat16)
    gate_grad = (hidden_grad * up_val * sigma * (1.0 + gate * (1.0 - sigma))).astype(jnp.bfloat16)
    return jnp.stack([hidden, gate_grad, up_grad])


def product(a, b, contract_a, contract_b):
    out = lax.dot_general(
        a, b, (((contract_a,), (contract_b,)), ((), ())), preferred_element_type=jnp.float32
    )
    return out.astype(jnp.bfloat16)


def forward_kernel(mine_ref, other_ref, tokens_ref, out_ref):
    width = mine_ref.shape[2]
    total = lax.dot_general(
        mine_ref[0], tokens_ref[:, :width], (((1,), (1,)), ((), ())),
        preferred_element_type=jnp.float32,
    ) + lax.dot_general(
        other_ref[0], tokens_ref[:, width:], (((1,), (1,)), ((), ())),
        preferred_element_type=jnp.float32,
    )
    rows = out_ref.shape[2]
    for part in range(out_ref.shape[0]):
        out_ref[part, 0] = total[part * rows : (part + 1) * rows].astype(out_ref.dtype)


def forward(mine, other, tokens):
    _, units, width = mine.shape
    half = tokens.shape[0]
    block = pl.BlockSpec((1, units, width), lambda i: (i, 0, 0))
    return pl.pallas_call(
        forward_kernel,
        grid=(3,),
        in_specs=[block, block, pl.BlockSpec((half, 2 * width), lambda i: (0, i // 2))],
        out_specs=pl.BlockSpec((Z, 1, units // Z, half), lambda i: (0, i, 0, 0)),
        out_shape=jax.ShapeDtypeStruct((Z, 3, units // Z, half), jnp.bfloat16),
        compiler_params=pltpu.CompilerParams(vmem_limit_bytes=16 * 1024 * 1024),
        cost_estimate=pl.CostEstimate(
            flops=12 * units * width * half, bytes_accessed=16 * units * width, transcendentals=0
        ),
        name="forward",
    )(mine, other, tokens)


def on_device(activations, out_grad, w_gate, w_up, w_down):
    tokens, width = activations.shape
    units = w_gate.shape[1]
    few = tokens // 2
    half = X * Y * few
    first = lax.axis_index("core") == 0

    sent = jnp.concatenate([activations, out_grad], axis=1).reshape(1, 2, few, 2 * width)
    sent = jnp.broadcast_to(sent, (Y, 2, few, 2 * width)).reshape(2 * Y, few, 2 * width)
    got = lax.all_to_all(sent, ("y", "core"), 0, 0).reshape(Y, 2, few, 2, width)
    own = jnp.where(first, got[:, 0], got[:, 1])
    other = jnp.where(first, got[:, 1], got[:, 0])
    block = jnp.concatenate([own[:, :, 0], other[:, :, 0], own[:, :, 1], other[:, :, 1]], axis=2)
    both = gather(block.reshape(Y * few, 4 * width), "x", X).reshape(half, 4 * width)

    weights = jnp.stack([w_gate.T, w_up.T, w_down])
    swapped = lax.ppermute(weights, "core", SWAP)
    wide = jnp.concatenate([weights[:2], swapped[:2]], axis=2)
    rows = units // Z
    sent = forward(weights, swapped, both)
    summed = jnp.sum(lax.all_to_all(sent, "z", 0, 0).astype(jnp.float32), axis=0)
    mine = swiglu_parts(summed[0], summed[1], summed[2])
    own = gather(mine, "z", Z).transpose(1, 0, 2, 3).reshape(3, units, half)
    pair = own[1:]

    term = product(pair.reshape(2 * units, half), wide[:2].reshape(2 * units, 2 * width), 0, 0)
    terms = lax.all_to_all(term.reshape(X * Y, few, 2 * width), ROW, 0, 0)
    total = jnp.sum(terms.astype(jnp.float32), axis=0).astype(jnp.bfloat16)
    other = lax.ppermute(total[:, width:], "core", SWAP)
    in_grad = jnp.where(
        first,
        jnp.concatenate([total[:, :width], other]),
        jnp.concatenate([other, total[:, :width]]),
    )

    others = lax.ppermute(
        jnp.concatenate([both[:, width : 2 * width], both[:, 3 * width :]], axis=1), "core", SWAP
    )
    inputs = jnp.concatenate([both[:, :width], others[:, :width]])
    grads = jnp.concatenate([both[:, 2 * width : 3 * width], others[:, width:]])
    hidden, gate_grad, up_grad = jnp.concatenate(
        [own, lax.ppermute(own, "core", SWAP)], axis=2
    )

    grad_down = product(hidden, grads, 1, 0)
    grad_gate = product(inputs, gate_grad, 0, 1)
    grad_up = product(inputs, up_grad, 0, 1)
    return (in_grad, grad_gate, grad_up, grad_down)


def solution(mesh):
    grid = Mesh(mesh.devices.reshape(X, Y, Z, 2), ROW + COL)
    return jax.shard_map(
        on_device,
        mesh=grid,
        in_specs=(P(ROW, COL), P(ROW, COL), P(COL, ROW), P(COL, ROW), P(ROW, COL)),
        out_specs=(P(ROW, COL), P(COL, ROW), P(COL, ROW), P(ROW, COL)),
        check_vma=False,
    )
```

```python
import jax
import jax.numpy as jnp
from jax import lax
from jax.experimental import pallas as pl
from jax.experimental.pallas import tpu as pltpu
from jax.sharding import Mesh
from jax.sharding import PartitionSpec as P

X, Y, Z = 4, 8, 8
ROW = ("x", "y")
COL = ("z", "core")
SWAP = ((0, 1), (1, 0))
PARAMS = pltpu.CompilerParams(vmem_limit_bytes=16 * 1024 * 1024)


def gather(block, axis, count):
    return lax.all_to_all(jnp.broadcast_to(block[None], (count,) + block.shape), axis, 0, 0)


def swiglu_parts(gate, up_val, hidden_grad):
    sigma = jax.nn.sigmoid(gate)
    hidden = (gate * sigma * up_val).astype(jnp.bfloat16)
    up_grad = (hidden_grad * gate * sigma).astype(jnp.bfloat16)
    gate_grad = (hidden_grad * up_val * sigma * (1.0 + gate * (1.0 - sigma))).astype(jnp.bfloat16)
    return jnp.stack([hidden, gate_grad, up_grad])


def product(a, b, contract_a, contract_b):
    return lax.dot_general(
        a, b, (((contract_a,), (contract_b,)), ((), ())), preferred_element_type=jnp.float32
    )


def cost(flops, bytes_accessed):
    return pl.CostEstimate(flops=flops, bytes_accessed=bytes_accessed, transcendentals=0)


def forward_kernel(mine_ref, other_ref, both_ref, out_ref):
    width = mine_ref.shape[2]
    rows = out_ref.shape[2]
    for i in range(3):
        at = i // 2 * width
        total = product(mine_ref[i], both_ref[:, at : at + width], 1, 1)
        at += 2 * width
        total = total + product(other_ref[i], both_ref[:, at : at + width], 1, 1)
        for part in range(out_ref.shape[0]):
            out_ref[part, i] = total[part * rows : (part + 1) * rows].astype(out_ref.dtype)


def forward(mine, other, both):
    _, units, width = mine.shape
    half = both.shape[0]
    whole = pl.BlockSpec(memory_space=pltpu.VMEM)
    return pl.pallas_call(
        forward_kernel,
        in_specs=[whole] * 3,
        out_specs=whole,
        out_shape=jax.ShapeDtypeStruct((Z, 3, units // Z, half), jnp.bfloat16),
        compiler_params=PARAMS,
        cost_estimate=cost(12 * units * width * half, 16 * units * width),
        name="forward",
    )(mine, other, both)


def backward_kernel(core_ref, mine_ref, other_ref, here_ref, there_ref, down_ref, gate_ref, up_ref):
    total = product(mine_ref[0], here_ref[...], 1, 0) + product(other_ref[0], there_ref[0], 1, 0)
    total = total.astype(jnp.bfloat16)
    for step, out_ref in enumerate((down_ref, gate_ref, up_ref)):

        @pl.when(pl.program_id(0) == step)
        def store(out_ref=out_ref):
            out_ref[...] = total


def backward(core, mine, other, both, others):
    _, units, half = mine.shape
    width = others.shape[2] // 2
    block = pl.BlockSpec((1, units, half), lambda i, core: (i, 0, 0))
    tokens = pl.BlockSpec((half, width), lambda i, core: (0, 1 - (i + 1) // 2))
    there = pl.BlockSpec(
        (1, half, width), lambda i, core: (1 - core[0], 0, 1 - (i + 1) // 2)
    )
    whole = jax.ShapeDtypeStruct((units, width), jnp.bfloat16)
    return pl.pallas_call(
        backward_kernel,
        grid_spec=pltpu.PrefetchScalarGridSpec(
            num_scalar_prefetch=1,
            grid=(3,),
            in_specs=[block, block, tokens, there],
            out_specs=[pl.BlockSpec((units, width), lambda i, core: (0, 0))] * 3,
        ),
        out_shape=[whole] * 3,
        compiler_params=PARAMS,
        cost_estimate=cost(12 * units * width * half, 16 * units * half),
        name="backward",
    )(core, mine, other, both, others)


def input_kernel(own_ref, mine_ref, other_ref, out_ref):
    width = mine_ref.shape[2]
    shape = out_ref.shape[:2] + (width,)
    for at, ref in ((0, mine_ref), (width, other_ref)):
        total = product(own_ref[1], ref[0], 0, 0) + product(own_ref[2], ref[1], 0, 0)
        out_ref[:, :, at : at + width] = total.reshape(shape).astype(out_ref.dtype)


def input_terms(own, mine, other):
    _, units, width = mine.shape
    half = own.shape[2]
    whole = pl.BlockSpec(memory_space=pltpu.VMEM)
    return pl.pallas_call(
        input_kernel,
        in_specs=[whole] * 3,
        out_specs=whole,
        out_shape=jax.ShapeDtypeStruct((X * Y, half // (X * Y), 2 * width), jnp.bfloat16),
        compiler_params=PARAMS,
        cost_estimate=cost(8 * units * width * half, 8 * units * width),
        name="input_terms",
    )(own, mine, other)


def on_device(activations, out_grad, w_gate, w_up, w_down):
    tokens, width = activations.shape
    units = w_gate.shape[1]
    few = tokens // 2
    half = X * Y * few
    rows = units // Z
    first = lax.axis_index("core") == 0

    sent = jnp.concatenate([activations, out_grad], axis=1).reshape(1, 2, few, 2 * width)
    sent = jnp.broadcast_to(sent, (Y, 2, few, 2 * width)).reshape(2 * Y, few, 2 * width)
    got = lax.all_to_all(sent, ("y", "core"), 0, 0).reshape(Y, 2, few, 2 * width)
    own = jnp.where(first, got[:, 0], got[:, 1])
    other = jnp.where(first, got[:, 1], got[:, 0])
    block = jnp.concatenate([own, other], axis=2).reshape(Y * few, 4 * width)
    both = gather(block, "x", X).reshape(half, 4 * width)

    weights = jnp.stack([w_gate.T, w_up.T, w_down])
    swapped = lax.ppermute(weights, "core", SWAP)

    sent = forward(weights, swapped, both)
    summed = jnp.sum(lax.all_to_all(sent, "z", 0, 0).astype(jnp.float32), axis=0)
    mine = swiglu_parts(summed[0], summed[1], summed[2])
    own = gather(mine, "z", Z).transpose(1, 0, 2, 3).reshape(3, units, half)

    term = input_terms(own, weights, swapped)
    terms = lax.all_to_all(term, ROW, 0, 0)
    total = jnp.sum(terms.astype(jnp.float32), axis=0).astype(jnp.bfloat16)
    pairs = lax.all_gather(total, "core", axis=0)
    in_grad = jnp.concatenate(
        [
            jnp.where(first, pairs[0, :, :width], pairs[0, :, width:]),
            jnp.where(first, pairs[1, :, width:], pairs[1, :, :width]),
        ]
    )


    others = jnp.concatenate(
        [
            lax.all_gather(both[:, 2 * width : 3 * width], "core", axis=0),
            lax.all_gather(both[:, 3 * width :], "core", axis=0),
        ],
        axis=2,
    )
    core = lax.axis_index("core").astype(jnp.int32).reshape(1)
    grad_down, grad_gate, grad_up = backward(core, own, lax.ppermute(own, "core", SWAP), both, others)
    grad_gate, grad_up = grad_gate.T, grad_up.T

    return (in_grad, grad_gate, grad_up, grad_down)


def solution(mesh):
    grid = Mesh(mesh.devices.reshape(X, Y, Z, 2), ROW + COL)
    return jax.shard_map(
        on_device,
        mesh=grid,
        in_specs=(P(ROW, COL), P(ROW, COL), P(COL, ROW), P(COL, ROW), P(ROW, COL)),
        out_specs=(P(ROW, COL), P(COL, ROW), P(COL, ROW), P(ROW, COL)),
        check_vma=False,
    )
```

```python
import jax
import jax.numpy as jnp
from jax import lax
from jax.experimental import pallas as pl
from jax.experimental.pallas import tpu as pltpu
from jax.sharding import Mesh
from jax.sharding import PartitionSpec as P

X, Y, Z = 4, 8, 8
ROW = ("x", "y")
COL = ("z", "core")
SWAP = ((0, 1), (1, 0))
PARAMS = pltpu.CompilerParams(vmem_limit_bytes=16 * 1024 * 1024)


def gather(block, axis, count):
    return lax.all_to_all(jnp.broadcast_to(block[None], (count,) + block.shape), axis, 0, 0)


def swiglu_parts(gate, up_val, hidden_grad):
    sigma = jax.nn.sigmoid(gate)
    hidden = (gate * sigma * up_val).astype(jnp.bfloat16)
    up_grad = (hidden_grad * gate * sigma).astype(jnp.bfloat16)
    gate_grad = (hidden_grad * up_val * sigma * (1.0 + gate * (1.0 - sigma))).astype(jnp.bfloat16)
    return jnp.stack([hidden, gate_grad, up_grad])


def product(a, b, contract_a, contract_b):
    return lax.dot_general(
        a, b, (((contract_a,), (contract_b,)), ((), ())), preferred_element_type=jnp.float32
    )


def cost(flops, bytes_accessed):
    return pl.CostEstimate(flops=flops, bytes_accessed=bytes_accessed, transcendentals=0)


def forward_kernel(core_ref, gate_ref, up_ref, down_ref, both_ref, out_ref):
    core = core_ref[0]
    width = gate_ref.shape[2]
    rows = out_ref.shape[2]
    for i, ref in enumerate((gate_ref, up_ref, down_ref)):
        at = i // 2 * width
        total = product(ref[core], both_ref[:, at : at + width], 1, 1)
        at += 2 * width
        total = total + product(ref[1 - core], both_ref[:, at : at + width], 1, 1)
        for part in range(out_ref.shape[0]):
            out_ref[part, i] = total[part * rows : (part + 1) * rows].astype(out_ref.dtype)


def forward(core, weights, both):
    _, units, width = weights[0].shape
    half = both.shape[0]
    whole = pl.BlockSpec(memory_space=pltpu.VMEM)
    return pl.pallas_call(
        forward_kernel,
        in_specs=[pl.BlockSpec(memory_space=pltpu.SMEM)] + [whole] * 4,
        out_specs=whole,
        out_shape=jax.ShapeDtypeStruct((Z, 3, units // Z, half), jnp.bfloat16),
        compiler_params=PARAMS,
        cost_estimate=cost(12 * units * width * half, 16 * units * width),
        name="forward",
    )(core, *weights, both)


def backward_kernel(core_ref, mine_ref, other_ref, here_ref, there_ref, down_ref, gate_ref, up_ref):
    total = product(mine_ref[0], here_ref[...], 1, 0) + product(other_ref[0], there_ref[0], 1, 0)
    total = total.astype(jnp.bfloat16)
    for step, out_ref in enumerate((down_ref, gate_ref, up_ref)):

        @pl.when(pl.program_id(0) == step)
        def store(out_ref=out_ref):
            out_ref[...] = total


def backward(core, mine, other, both, others):
    _, units, half = mine.shape
    width = others.shape[2] // 2
    block = pl.BlockSpec((1, units, half), lambda i, core: (i, 0, 0))
    tokens = pl.BlockSpec((half, width), lambda i, core: (0, 1 - (i + 1) // 2))
    there = pl.BlockSpec(
        (1, half, width), lambda i, core: (1 - core[0], 0, 1 - (i + 1) // 2)
    )
    whole = jax.ShapeDtypeStruct((units, width), jnp.bfloat16)
    return pl.pallas_call(
        backward_kernel,
        grid_spec=pltpu.PrefetchScalarGridSpec(
            num_scalar_prefetch=1,
            grid=(3,),
            in_specs=[block, block, tokens, there],
            out_specs=[pl.BlockSpec((units, width), lambda i, core: (0, 0))] * 3,
        ),
        out_shape=[whole] * 3,
        compiler_params=PARAMS,
        cost_estimate=cost(12 * units * width * half, 16 * units * half),
        name="backward",
    )(core, mine, other, both, others)


def input_kernel(core_ref, own_ref, gate_ref, up_ref, out_ref, block_ref, sent_ref):
    core = core_ref[0]
    width = gate_ref.shape[2]
    copies = []
    for i, side in enumerate((core, 1 - core)):
        total = product(own_ref[1], gate_ref[side], 0, 0) + product(own_ref[2], up_ref[side], 0, 0)
        block_ref[i] = total.astype(block_ref.dtype)
        lanes = pl.ds(i * width, width)
        copies.append(
            pltpu.make_async_copy(block_ref.at[i], out_ref.at[:, lanes], sent_ref.at[i])
        )
        copies[i].start()
    for copy in copies:
        copy.wait()


def input_terms(core, own, weights):
    _, units, width = weights[0].shape
    half = own.shape[2]
    whole = pl.BlockSpec(memory_space=pltpu.VMEM)
    return pl.pallas_call(
        input_kernel,
        in_specs=[pl.BlockSpec(memory_space=pltpu.SMEM)] + [whole] * 3,
        out_specs=pl.BlockSpec(memory_space=pltpu.HBM),
        out_shape=jax.ShapeDtypeStruct((half, 2 * width), jnp.bfloat16),
        scratch_shapes=[
            pltpu.VMEM((2, half, width), jnp.bfloat16),
            pltpu.SemaphoreType.DMA((2,)),
        ],
        compiler_params=PARAMS,
        cost_estimate=cost(8 * units * width * half, 8 * units * width),
        name="input_terms",
    )(core, own, *weights[:2])


def on_device(activations, out_grad, w_gate, w_up, w_down):
    tokens, width = activations.shape
    units = w_gate.shape[1]
    few = tokens // 2
    half = X * Y * few
    rows = units // Z
    first = lax.axis_index("core") == 0

    sent = jnp.concatenate([activations, out_grad], axis=1).reshape(1, 2, few, 2 * width)
    sent = jnp.broadcast_to(sent, (Y, 2, few, 2 * width)).reshape(2 * Y, few, 2 * width)
    got = lax.all_to_all(sent, ("y", "core"), 0, 0).reshape(Y, 2, few, 2 * width)
    own = jnp.where(first, got[:, 0], got[:, 1])
    other = jnp.where(first, got[:, 1], got[:, 0])
    block = jnp.concatenate([own, other], axis=2).reshape(Y * few, 4 * width)
    core = lax.axis_index("core").astype(jnp.int32).reshape(1)
    weights = [lax.all_gather(w, "core", axis=0) for w in (w_gate.T, w_up.T, w_down)]
    block, weights = lax.optimization_barrier((block, weights))
    both = gather(block, "x", X).reshape(half, 4 * width)

    sent = forward(core, weights, both)
    summed = jnp.sum(lax.all_to_all(sent, "z", 0, 0).astype(jnp.float32), axis=0)
    mine = swiglu_parts(summed[0], summed[1], summed[2])
    own = gather(mine, "z", Z).transpose(1, 0, 2, 3).reshape(3, units, half)

    term = input_terms(core, own, weights)
    terms = lax.all_to_all(term.reshape(X * Y, few, 2 * width), ROW, 0, 0)
    total = jnp.sum(terms.astype(jnp.float32), axis=0).astype(jnp.bfloat16)
    pairs = lax.all_gather(total, "core", axis=0)
    in_grad = jnp.concatenate(
        [
            jnp.where(first, pairs[0, :, :width], pairs[0, :, width:]),
            jnp.where(first, pairs[1, :, width:], pairs[1, :, :width]),
        ]
    )


    others = jnp.concatenate(
        [
            lax.all_gather(both[:, 2 * width : 3 * width], "core", axis=0),
            lax.all_gather(both[:, 3 * width :], "core", axis=0),
        ],
        axis=2,
    )
    grad_down, grad_gate, grad_up = backward(core, own, lax.ppermute(own, "core", SWAP), both, others)
    grad_gate, grad_up = grad_gate.T, grad_up.T

    return (in_grad, grad_gate, grad_up, grad_down)


def solution(mesh):
    grid = Mesh(mesh.devices.reshape(X, Y, Z, 2), ROW + COL)
    return jax.shard_map(
        on_device,
        mesh=grid,
        in_specs=(P(ROW, COL), P(ROW, COL), P(COL, ROW), P(COL, ROW), P(ROW, COL)),
        out_specs=(P(ROW, COL), P(COL, ROW), P(COL, ROW), P(ROW, COL)),
        check_vma=False,
    )
```

```python
import jax
import jax.numpy as jnp
from jax import lax
from jax.experimental import pallas as pl
from jax.experimental.pallas import tpu as pltpu
from jax.sharding import Mesh
from jax.sharding import PartitionSpec as P

X, Y, Z = 4, 8, 8
ROW = ("x", "y")
COL = ("z", "core")
SWAP = ((0, 1), (1, 0))
PARAMS = pltpu.CompilerParams(vmem_limit_bytes=16 * 1024 * 1024)


def gather(block, axis, count):
    return lax.all_to_all(jnp.broadcast_to(block[None], (count,) + block.shape), axis, 0, 0)


def swiglu_parts(gate, up_val, hidden_grad):
    sigma = jax.nn.sigmoid(gate)
    hidden = (gate * sigma * up_val).astype(jnp.bfloat16)
    up_grad = (hidden_grad * gate * sigma).astype(jnp.bfloat16)
    gate_grad = (hidden_grad * up_val * sigma * (1.0 + gate * (1.0 - sigma))).astype(jnp.bfloat16)
    return jnp.stack([hidden, gate_grad, up_grad])


def product(a, b, contract_a, contract_b):
    return lax.dot_general(
        a, b, (((contract_a,), (contract_b,)), ((), ())), preferred_element_type=jnp.float32
    )


def cost(flops, bytes_accessed):
    return pl.CostEstimate(flops=flops, bytes_accessed=bytes_accessed, transcendentals=0)


def forward_kernel(core_ref, gate_ref, up_ref, down_ref, both_ref, out_ref):
    core = core_ref[0]
    width = gate_ref.shape[2]
    rows = out_ref.shape[2]
    for i, ref in enumerate((gate_ref, up_ref, down_ref)):
        at = i // 2 * width
        total = product(ref[core], both_ref[:, at : at + width], 1, 1)
        at += 2 * width
        total = total + product(ref[1 - core], both_ref[:, at : at + width], 1, 1)
        for part in range(out_ref.shape[0]):
            out_ref[part, i] = total[part * rows : (part + 1) * rows].astype(out_ref.dtype)


def forward(core, weights, both):
    _, units, width = weights[0].shape
    half = both.shape[0]
    whole = pl.BlockSpec(memory_space=pltpu.VMEM)
    return pl.pallas_call(
        forward_kernel,
        in_specs=[pl.BlockSpec(memory_space=pltpu.SMEM)] + [whole] * 4,
        out_specs=whole,
        out_shape=jax.ShapeDtypeStruct((Z, 3, units // Z, half), jnp.bfloat16),
        compiler_params=PARAMS,
        cost_estimate=cost(12 * units * width * half, 16 * units * width),
        name="forward",
    )(core, *weights, both)


def backward_kernel(core_ref, mine_ref, other_ref, here_ref, there_ref, down_ref, gate_ref, up_ref):
    total = product(mine_ref[0], here_ref[...], 1, 0) + product(other_ref[0], there_ref[0], 1, 0)
    total = total.astype(jnp.bfloat16)
    for step, out_ref in enumerate((down_ref, gate_ref, up_ref)):

        @pl.when(pl.program_id(0) == step)
        def store(out_ref=out_ref):
            out_ref[...] = total


def backward(core, mine, other, both, others):
    _, units, half = mine.shape
    width = others.shape[2] // 2
    block = pl.BlockSpec((1, units, half), lambda i, core: (i, 0, 0))
    tokens = pl.BlockSpec((half, width), lambda i, core: (0, 1 - (i + 1) // 2))
    there = pl.BlockSpec(
        (1, half, width), lambda i, core: (1 - core[0], 0, 1 - (i + 1) // 2)
    )
    whole = jax.ShapeDtypeStruct((units, width), jnp.bfloat16)
    return pl.pallas_call(
        backward_kernel,
        grid_spec=pltpu.PrefetchScalarGridSpec(
            num_scalar_prefetch=1,
            grid=(3,),
            in_specs=[block, block, tokens, there],
            out_specs=[pl.BlockSpec((units, width), lambda i, core: (0, 0))] * 3,
        ),
        out_shape=[whole] * 3,
        compiler_params=PARAMS,
        cost_estimate=cost(12 * units * width * half, 16 * units * half),
        name="backward",
    )(core, mine, other, both, others)


def input_kernel(core_ref, own_ref, gate_ref, up_ref, out_ref, block_ref, sent_ref):
    core = core_ref[0]
    width = gate_ref.shape[2]
    copies = []
    for i, side in enumerate((core, 1 - core)):
        total = product(own_ref[1], gate_ref[side], 0, 0) + product(own_ref[2], up_ref[side], 0, 0)
        block_ref[i] = total.astype(block_ref.dtype)
        lanes = pl.ds(i * width, width)
        copies.append(
            pltpu.make_async_copy(block_ref.at[i], out_ref.at[:, lanes], sent_ref.at[i])
        )
        copies[i].start()
    for copy in copies:
        copy.wait()


def input_terms(core, own, weights):
    _, units, width = weights[0].shape
    half = own.shape[2]
    whole = pl.BlockSpec(memory_space=pltpu.VMEM)
    return pl.pallas_call(
        input_kernel,
        in_specs=[pl.BlockSpec(memory_space=pltpu.SMEM)] + [whole] * 3,
        out_specs=pl.BlockSpec(memory_space=pltpu.HBM),
        out_shape=jax.ShapeDtypeStruct((half, 2 * width), jnp.bfloat16),
        scratch_shapes=[
            pltpu.VMEM((2, half, width), jnp.bfloat16),
            pltpu.SemaphoreType.DMA((2,)),
        ],
        compiler_params=PARAMS,
        cost_estimate=cost(8 * units * width * half, 8 * units * width),
        name="input_terms",
    )(core, own, *weights[:2])


def on_device(activations, out_grad, w_gate, w_up, w_down):
    tokens, width = activations.shape
    units = w_gate.shape[1]
    few = tokens // 2
    half = X * Y * few
    rows = units // Z
    first = lax.axis_index("core") == 0

    sent = jnp.concatenate([activations, out_grad], axis=1).reshape(2, 1, few, 2 * width)
    sent = jnp.broadcast_to(sent, (2, Y, few, 2 * width)).reshape(2 * Y, few, 2 * width)
    got = lax.all_to_all(sent, ("core", "y"), 0, 0).reshape(2, Y, few, 2 * width)
    own = jnp.where(first, got[0], got[1])
    other = jnp.where(first, got[1], got[0])
    block = jnp.concatenate([own, other], axis=2).reshape(Y * few, 4 * width)
    core = lax.axis_index("core").astype(jnp.int32).reshape(1)
    weights = [lax.all_gather(w, "core", axis=0) for w in (w_gate.T, w_up.T, w_down)]
    block, weights = lax.optimization_barrier((block, weights))
    both = gather(block, "x", X).reshape(half, 4 * width)

    sent = forward(core, weights, both)
    summed = jnp.sum(lax.all_to_all(sent, "z", 0, 0).astype(jnp.float32), axis=0)
    mine = swiglu_parts(summed[0], summed[1], summed[2])
    own = gather(mine, "z", Z).transpose(1, 0, 2, 3).reshape(3, units, half)

    term = input_terms(core, own, weights)
    terms = lax.all_to_all(term.reshape(X * Y, few, 2 * width), ROW, 0, 0)
    total = jnp.sum(terms.astype(jnp.float32), axis=0).astype(jnp.bfloat16)
    pairs = lax.all_gather(total, "core", axis=0)
    in_grad = jnp.concatenate(
        [
            jnp.where(first, pairs[0, :, :width], pairs[0, :, width:]),
            jnp.where(first, pairs[1, :, width:], pairs[1, :, :width]),
        ]
    )


    others = jnp.concatenate(
        [
            lax.all_gather(both[:, 2 * width : 3 * width], "core", axis=0),
            lax.all_gather(both[:, 3 * width :], "core", axis=0),
        ],
        axis=2,
    )
    grad_down, grad_gate, grad_up = backward(core, own, lax.ppermute(own, "core", SWAP), both, others)
    grad_gate, grad_up = grad_gate.T, grad_up.T

    return (in_grad, grad_gate, grad_up, grad_down)


def solution(mesh):
    grid = Mesh(mesh.devices.reshape(X, Y, Z, 2), ROW + COL)
    return jax.shard_map(
        on_device,
        mesh=grid,
        in_specs=(P(ROW, COL), P(ROW, COL), P(COL, ROW), P(COL, ROW), P(ROW, COL)),
        out_specs=(P(ROW, COL), P(COL, ROW), P(COL, ROW), P(ROW, COL)),
        check_vma=False,
    )
```

```python
import jax
import jax.numpy as jnp
from jax import lax
from jax.experimental import pallas as pl
from jax.experimental.pallas import tpu as pltpu
from jax.sharding import Mesh
from jax.sharding import PartitionSpec as P

X, Y, Z = 4, 8, 8
ROW = ("x", "y_high", "y_low")
COL = ("z_high", "z_low", "core")
Y_PEERS = ("y_low", "y_high")
Z_PEERS = ("z_low", "z_high")
SWAP = ((0, 1), (1, 0))
PARAMS = pltpu.CompilerParams(vmem_limit_bytes=16 * 1024 * 1024)


def gather(block, axis, count):
    return lax.all_to_all(jnp.broadcast_to(block[None], (count,) + block.shape), axis, 0, 0)


def swiglu_parts(gate, up_val, hidden_grad):
    sigma = jax.nn.sigmoid(gate)
    hidden = (gate * sigma * up_val).astype(jnp.bfloat16)
    up_grad = (hidden_grad * gate * sigma).astype(jnp.bfloat16)
    gate_grad = (hidden_grad * up_val * sigma * (1.0 + gate * (1.0 - sigma))).astype(jnp.bfloat16)
    return jnp.stack([hidden, gate_grad, up_grad])


def product(a, b, contract_a, contract_b):
    return lax.dot_general(
        a, b, (((contract_a,), (contract_b,)), ((), ())), preferred_element_type=jnp.float32
    )


def cost(flops, bytes_accessed):
    return pl.CostEstimate(flops=flops, bytes_accessed=bytes_accessed, transcendentals=0)


def forward_kernel(core_ref, gate_ref, up_ref, down_ref, both_ref, out_ref):
    core = core_ref[0]
    width = gate_ref.shape[2]
    rows = out_ref.shape[2]
    for i, ref in enumerate((gate_ref, up_ref, down_ref)):
        at = i // 2 * width
        total = product(ref[core], both_ref[:, at : at + width], 1, 1)
        at += 2 * width
        total = total + product(ref[1 - core], both_ref[:, at : at + width], 1, 1)
        for part in range(out_ref.shape[0]):
            out_ref[part, i] = total[part * rows : (part + 1) * rows].astype(out_ref.dtype)


def forward(core, weights, both):
    _, units, width = weights[0].shape
    half = both.shape[0]
    whole = pl.BlockSpec(memory_space=pltpu.VMEM)
    return pl.pallas_call(
        forward_kernel,
        in_specs=[pl.BlockSpec(memory_space=pltpu.SMEM)] + [whole] * 4,
        out_specs=whole,
        out_shape=jax.ShapeDtypeStruct((Z, 3, units // Z, half), jnp.bfloat16),
        compiler_params=PARAMS,
        cost_estimate=cost(12 * units * width * half, 16 * units * width),
        name="forward",
    )(core, *weights, both)


def backward_kernel(core_ref, mine_ref, other_ref, here_ref, there_ref, down_ref, gate_ref, up_ref):
    total = product(mine_ref[0], here_ref[...], 1, 0) + product(other_ref[0], there_ref[0], 1, 0)
    total = total.astype(jnp.bfloat16)
    for step, out_ref in enumerate((down_ref, gate_ref, up_ref)):

        @pl.when(pl.program_id(0) == step)
        def store(out_ref=out_ref):
            out_ref[...] = total


def backward(core, mine, other, both, others):
    _, units, half = mine.shape
    width = others.shape[2] // 2
    block = pl.BlockSpec((1, units, half), lambda i, core: (i, 0, 0))
    tokens = pl.BlockSpec((half, width), lambda i, core: (0, 1 - (i + 1) // 2))
    there = pl.BlockSpec(
        (1, half, width), lambda i, core: (1 - core[0], 0, 1 - (i + 1) // 2)
    )
    whole = jax.ShapeDtypeStruct((units, width), jnp.bfloat16)
    return pl.pallas_call(
        backward_kernel,
        grid_spec=pltpu.PrefetchScalarGridSpec(
            num_scalar_prefetch=1,
            grid=(3,),
            in_specs=[block, block, tokens, there],
            out_specs=[pl.BlockSpec((units, width), lambda i, core: (0, 0))] * 3,
        ),
        out_shape=[whole] * 3,
        compiler_params=PARAMS,
        cost_estimate=cost(12 * units * width * half, 16 * units * half),
        name="backward",
    )(core, mine, other, both, others)


def input_kernel(core_ref, own_ref, gate_ref, up_ref, out_ref, block_ref, sent_ref):
    core = core_ref[0]
    width = gate_ref.shape[2]
    copies = []
    for i, side in enumerate((core, 1 - core)):
        total = product(own_ref[1], gate_ref[side], 0, 0) + product(own_ref[2], up_ref[side], 0, 0)
        block_ref[i] = total.astype(block_ref.dtype)
        lanes = pl.ds(i * width, width)
        copies.append(
            pltpu.make_async_copy(block_ref.at[i], out_ref.at[:, lanes], sent_ref.at[i])
        )
        copies[i].start()
    for copy in copies:
        copy.wait()


def input_terms(core, own, weights):
    _, units, width = weights[0].shape
    half = own.shape[2]
    whole = pl.BlockSpec(memory_space=pltpu.VMEM)
    return pl.pallas_call(
        input_kernel,
        in_specs=[pl.BlockSpec(memory_space=pltpu.SMEM)] + [whole] * 3,
        out_specs=pl.BlockSpec(memory_space=pltpu.HBM),
        out_shape=jax.ShapeDtypeStruct((half, 2 * width), jnp.bfloat16),
        scratch_shapes=[
            pltpu.VMEM((2, half, width), jnp.bfloat16),
            pltpu.SemaphoreType.DMA((2,)),
        ],
        compiler_params=PARAMS,
        cost_estimate=cost(8 * units * width * half, 8 * units * width),
        name="input_terms",
    )(core, own, *weights[:2])


def on_device(activations, out_grad, w_gate, w_up, w_down):
    tokens, width = activations.shape
    units = w_gate.shape[1]
    few = tokens // 2
    half = X * Y * few
    rows = units // Z
    first = lax.axis_index("core") == 0

    sent = jnp.concatenate([activations, out_grad], axis=1).reshape(2, 1, few, 2 * width)
    sent = jnp.broadcast_to(sent, (2, Y, few, 2 * width)).reshape(2 * Y, few, 2 * width)
    got = lax.all_to_all(sent, ("core",) + Y_PEERS, 0, 0).reshape(2, Y, few, 2 * width)
    own = jnp.where(first, got[0], got[1])
    other = jnp.where(first, got[1], got[0])
    block = jnp.concatenate([own, other], axis=2).reshape(Y * few, 4 * width)
    core = lax.axis_index("core").astype(jnp.int32).reshape(1)
    weights = [lax.all_gather(w, "core", axis=0) for w in (w_gate.T, w_up.T, w_down)]
    block, weights = lax.optimization_barrier((block, weights))
    both = gather(block, "x", X).reshape(half, 4 * width)

    sent = forward(core, weights, both)
    summed = jnp.sum(lax.all_to_all(sent, Z_PEERS, 0, 0).astype(jnp.float32), axis=0)
    mine = swiglu_parts(summed[0], summed[1], summed[2])
    own = gather(mine, Z_PEERS, Z).transpose(1, 0, 2, 3).reshape(3, units, half)

    term = input_terms(core, own, weights)
    terms = lax.all_to_all(term.reshape(X * Y, few, 2 * width), ("x",) + Y_PEERS, 0, 0)
    total = jnp.sum(terms.astype(jnp.float32), axis=0).astype(jnp.bfloat16)
    pairs = lax.all_gather(total, "core", axis=0)
    in_grad = jnp.concatenate(
        [
            jnp.where(first, pairs[0, :, :width], pairs[0, :, width:]),
            jnp.where(first, pairs[1, :, width:], pairs[1, :, :width]),
        ]
    )


    others = jnp.concatenate(
        [
            lax.all_gather(both[:, 2 * width : 3 * width], "core", axis=0),
            lax.all_gather(both[:, 3 * width :], "core", axis=0),
        ],
        axis=2,
    )
    grad_down, grad_gate, grad_up = backward(core, own, lax.ppermute(own, "core", SWAP), both, others)
    grad_gate, grad_up = grad_gate.T, grad_up.T

    return (in_grad, grad_gate, grad_up, grad_down)


def solution(mesh):
    grid = Mesh(mesh.devices.reshape(X, 2, Y // 2, 2, Z // 2, 2), ROW + COL)
    return jax.shard_map(
        on_device,
        mesh=grid,
        in_specs=(P(ROW, COL), P(ROW, COL), P(COL, ROW), P(COL, ROW), P(ROW, COL)),
        out_specs=(P(ROW, COL), P(COL, ROW), P(COL, ROW), P(ROW, COL)),
        check_vma=False,
    )
```

```python
import jax
import jax.numpy as jnp
from jax import lax
from jax.experimental import pallas as pl
from jax.experimental.pallas import tpu as pltpu
from jax.sharding import Mesh
from jax.sharding import PartitionSpec as P

X, Y, Z = 4, 8, 8
ROW = ("x1", "x0", "y2", "y1", "y0")
COL = ("z2", "z1", "z0", "core")
X_PEERS = ("x1", "x0")
Y_PEERS = ("y1", "y0", "y2")
Z_PEERS = ("z1", "z2", "z0")
SWAP = ((0, 1), (1, 0))
PARAMS = pltpu.CompilerParams(vmem_limit_bytes=16 * 1024 * 1024)


def gather(block, axis, count):
    return lax.all_to_all(jnp.broadcast_to(block[None], (count,) + block.shape), axis, 0, 0)


def swiglu_parts(gate, up_val, hidden_grad):
    sigma = jax.nn.sigmoid(gate)
    hidden = (gate * sigma * up_val).astype(jnp.bfloat16)
    up_grad = (hidden_grad * gate * sigma).astype(jnp.bfloat16)
    gate_grad = (hidden_grad * up_val * sigma * (1.0 + gate * (1.0 - sigma))).astype(jnp.bfloat16)
    return jnp.stack([hidden, gate_grad, up_grad])


def product(a, b, contract_a, contract_b):
    return lax.dot_general(
        a, b, (((contract_a,), (contract_b,)), ((), ())), preferred_element_type=jnp.float32
    )


def cost(flops, bytes_accessed):
    return pl.CostEstimate(flops=flops, bytes_accessed=bytes_accessed, transcendentals=0)


def forward_kernel(core_ref, gate_ref, up_ref, down_ref, both_ref, out_ref):
    core = core_ref[0]
    width = gate_ref.shape[2]
    rows = out_ref.shape[2]
    for i, ref in enumerate((gate_ref, up_ref, down_ref)):
        at = i // 2 * width
        total = product(ref[core], both_ref[:, at : at + width], 1, 1)
        at += 2 * width
        total = total + product(ref[1 - core], both_ref[:, at : at + width], 1, 1)
        for part in range(out_ref.shape[0]):
            out_ref[part, i] = total[part * rows : (part + 1) * rows].astype(out_ref.dtype)


def forward(core, weights, both):
    _, units, width = weights[0].shape
    half = both.shape[0]
    whole = pl.BlockSpec(memory_space=pltpu.VMEM)
    return pl.pallas_call(
        forward_kernel,
        in_specs=[pl.BlockSpec(memory_space=pltpu.SMEM)] + [whole] * 4,
        out_specs=whole,
        out_shape=jax.ShapeDtypeStruct((Z, 3, units // Z, half), jnp.bfloat16),
        compiler_params=PARAMS,
        cost_estimate=cost(12 * units * width * half, 16 * units * width),
        name="forward",
    )(core, *weights, both)


def backward_kernel(core_ref, mine_ref, other_ref, here_ref, there_ref, down_ref, gate_ref, up_ref):
    total = product(mine_ref[0], here_ref[...], 1, 0) + product(other_ref[0], there_ref[0], 1, 0)
    total = total.astype(jnp.bfloat16)
    for step, out_ref in enumerate((down_ref, gate_ref, up_ref)):

        @pl.when(pl.program_id(0) == step)
        def store(out_ref=out_ref):
            out_ref[...] = total


def backward(core, mine, other, both, others):
    _, units, half = mine.shape
    width = others.shape[2] // 2
    block = pl.BlockSpec((1, units, half), lambda i, core: (i, 0, 0))
    tokens = pl.BlockSpec((half, width), lambda i, core: (0, 1 - (i + 1) // 2))
    there = pl.BlockSpec(
        (1, half, width), lambda i, core: (1 - core[0], 0, 1 - (i + 1) // 2)
    )
    whole = jax.ShapeDtypeStruct((units, width), jnp.bfloat16)
    return pl.pallas_call(
        backward_kernel,
        grid_spec=pltpu.PrefetchScalarGridSpec(
            num_scalar_prefetch=1,
            grid=(3,),
            in_specs=[block, block, tokens, there],
            out_specs=[pl.BlockSpec((units, width), lambda i, core: (0, 0))] * 3,
        ),
        out_shape=[whole] * 3,
        compiler_params=PARAMS,
        cost_estimate=cost(12 * units * width * half, 16 * units * half),
        name="backward",
    )(core, mine, other, both, others)


def input_kernel(core_ref, own_ref, gate_ref, up_ref, out_ref, block_ref, sent_ref):
    core = core_ref[0]
    width = gate_ref.shape[2]
    copies = []
    for i, side in enumerate((core, 1 - core)):
        total = product(own_ref[1], gate_ref[side], 0, 0) + product(own_ref[2], up_ref[side], 0, 0)
        block_ref[i] = total.astype(block_ref.dtype)
        lanes = pl.ds(i * width, width)
        copies.append(
            pltpu.make_async_copy(block_ref.at[i], out_ref.at[:, lanes], sent_ref.at[i])
        )
        copies[i].start()
    for copy in copies:
        copy.wait()


def input_terms(core, own, weights):
    _, units, width = weights[0].shape
    half = own.shape[2]
    whole = pl.BlockSpec(memory_space=pltpu.VMEM)
    return pl.pallas_call(
        input_kernel,
        in_specs=[pl.BlockSpec(memory_space=pltpu.SMEM)] + [whole] * 3,
        out_specs=pl.BlockSpec(memory_space=pltpu.HBM),
        out_shape=jax.ShapeDtypeStruct((half, 2 * width), jnp.bfloat16),
        scratch_shapes=[
            pltpu.VMEM((2, half, width), jnp.bfloat16),
            pltpu.SemaphoreType.DMA((2,)),
        ],
        compiler_params=PARAMS,
        cost_estimate=cost(8 * units * width * half, 8 * units * width),
        name="input_terms",
    )(core, own, *weights[:2])


def on_device(activations, out_grad, w_gate, w_up, w_down):
    tokens, width = activations.shape
    units = w_gate.shape[1]
    few = tokens // 2
    half = X * Y * few
    rows = units // Z
    first = lax.axis_index("core") == 0

    sent = jnp.concatenate([activations, out_grad], axis=1).reshape(2, 1, few, 2 * width)
    sent = jnp.broadcast_to(sent, (2, Y, few, 2 * width)).reshape(2 * Y, few, 2 * width)
    got = lax.all_to_all(sent, ("core",) + Y_PEERS, 0, 0).reshape(2, Y, few, 2 * width)
    own = jnp.where(first, got[0], got[1])
    other = jnp.where(first, got[1], got[0])
    block = jnp.concatenate([own, other], axis=2).reshape(Y * few, 4 * width)
    core = lax.axis_index("core").astype(jnp.int32).reshape(1)
    weights = [lax.all_gather(w, "core", axis=0) for w in (w_gate.T, w_up.T, w_down)]
    block, weights = lax.optimization_barrier((block, weights))
    both = gather(block, X_PEERS, X).reshape(half, 4 * width)

    sent = forward(core, weights, both)
    summed = jnp.sum(lax.all_to_all(sent, Z_PEERS, 0, 0).astype(jnp.float32), axis=0)
    mine = swiglu_parts(summed[0], summed[1], summed[2])
    own = gather(mine, Z_PEERS, Z).transpose(1, 0, 2, 3).reshape(3, units, half)

    term = input_terms(core, own, weights)
    terms = lax.all_to_all(term.reshape(X * Y, few, 2 * width), X_PEERS + Y_PEERS, 0, 0)
    total = jnp.sum(terms.astype(jnp.float32), axis=0).astype(jnp.bfloat16)
    pairs = lax.all_gather(total, "core", axis=0)
    in_grad = jnp.concatenate(
        [
            jnp.where(first, pairs[0, :, :width], pairs[0, :, width:]),
            jnp.where(first, pairs[1, :, width:], pairs[1, :, :width]),
        ]
    )


    others = jnp.concatenate(
        [
            lax.all_gather(both[:, 2 * width : 3 * width], "core", axis=0),
            lax.all_gather(both[:, 3 * width :], "core", axis=0),
        ],
        axis=2,
    )
    grad_down, grad_gate, grad_up = backward(core, own, lax.ppermute(own, "core", SWAP), both, others)
    grad_gate, grad_up = grad_gate.T, grad_up.T

    return (in_grad, grad_gate, grad_up, grad_down)


def solution(mesh):
    grid = Mesh(mesh.devices.reshape((2,) * 9), ROW + COL)
    return jax.shard_map(
        on_device,
        mesh=grid,
        in_specs=(P(ROW, COL), P(ROW, COL), P(COL, ROW), P(COL, ROW), P(ROW, COL)),
        out_specs=(P(ROW, COL), P(COL, ROW), P(COL, ROW), P(ROW, COL)),
        check_vma=False,
    )
```
